32 devices in a mesh: branch: 2 (over core), seq: 4 (over y, x), rep: 4 (over z).
Axes of the slice: x: 2, y: 2, z: 4, core: 2. Of those that a mesh axis runs over, the one named last changes fastest.
Arguments:
- queries: bfloat16 [2, 2048, 2048], P('branch', ('rep', 'seq')), parts along dimension 1, may hold values from -64 to 64
- key_vecs: bfloat16 [2, 2048, 2048], P('branch', ('rep', 'seq')), parts along dimension 1, may hold values from -8 to 8
- value_vecs: bfloat16 [2, 2048, 2048], P('branch', ('rep', 'seq')), parts along dimension 1, may hold values from -6 to 6
- hidden_in: bfloat16 [2, 2048, 2048], P('branch', ('rep', 'seq')), parts along dimension 1, may hold values from -4 to 4
- out_proj: bfloat16 [2, 2048, 2048], P('branch', 'seq'), may hold values from -0.125 to 0.125
- couple_proj: bfloat16 [2, 2048, 2048], P('branch', 'seq'), may hold values from -0.125 to 0.125
- grad_mixed: bfloat16 [2, 2048, 2048], P('branch', ('rep', 'seq')), parts along dimension 1, may hold values from -6 to 6
Outputs:
- mixed_out: bfloat16 [2, 2048, 2048], P('branch', ('rep', 'seq')), parts along dimension 1
- grad_hidden: bfloat16 [2, 2048, 2048], P('branch', ('rep', 'seq')), parts along dimension 1
- grad_queries: bfloat16 [2, 2048, 2048], P('branch', ('rep', 'seq')), parts along dimension 1
- grad_keys: bfloat16 [2, 2048, 2048], P('branch', ('rep', 'seq')), parts along dimension 1
- grad_values: bfloat16 [2, 2048, 2048], P('branch', ('rep', 'seq')), parts along dimension 1
- grad_couple: float32 [2, 2048, 8192], P('branch', 'seq', 'rep'), parts along dimension 2
The draws below stay inside these ranges and needn't reach their ends.
There are 4 independent parts, one for each index of `rep`. The reference program is written for one: setup_inputs(seed, part) draws one part's arguments, and reference() takes and returns one part's arrays. A program takes and returns all parts, laid end to end along the dimension named above; an argument that names none is the same for every part. Nothing has to cross between parts.
All inputs are finite; a program needn't handle non-finite values.
Results may differ from the reference program's by a relative error of at most 0.015.
Values may be sent and summed in bfloat16 or wider, within the bound.
A program may use at most 128 MiB of HBM per device.

```python
import math
import jax
import jax.numpy as jnp
from jax import lax

D = 2048
NH = 16
HEAD = 128
S_DEV = 128
SEQ_LEN = 512
HE = 2048
HGROUP = 4
N_SEQ = 4


def paired_draw(key):
    shape_full = (2, SEQ_LEN, NH * HEAD)
    base_keys = jnp.clip(jax.random.normal(jax.random.fold_in(key, 101), shape_full, jnp.float32), -4.0, 4.0) * 1.5
    base_queries = jnp.clip(jax.random.normal(jax.random.fold_in(key, 102), shape_full, jnp.float32), -4.0, 4.0) * 1.5
    return (base_queries, base_keys)


def draw_queries(key, part):
    return paired_draw(key)[0].astype(jnp.bfloat16)


def draw_key_vecs(key, part):
    return paired_draw(key)[1].astype(jnp.bfloat16)


def level_of(stream_key, shape, pieces, low, high):
    gain = 1.0
    for dim, shards_of in pieces:
        heights = jax.random.uniform(jax.random.fold_in(jax.random.fold_in(stream_key, 6), dim), (shards_of,), jnp.float32, low / len(pieces), high / len(pieces))
        gain = gain * jnp.repeat(jnp.exp(heights), shape[dim] // shards_of).reshape((-1,) + (1,) * (len(shape) - 1 - dim))
    return gain


def centred(rng, extent, spread, most, shards=(), held_as=jnp.bfloat16):
    values = jax.random.normal(rng, extent, jnp.float32) * spread
    if len(shards) > 0:
        values = level_of(rng, extent, shards, -0.22, 0.18) * values
    return jnp.clip(values, min=-most, max=most).astype(held_as)


def setup_inputs(seed: int = 0, part: int = 0) -> dict:
    keys = jax.random.split(jax.random.key(seed), 8)
    part_keys = jax.random.split(jax.random.fold_in(keys[7], part), 8)
    return {
        "queries": draw_queries(jax.random.fold_in(jax.random.fold_in(keys[7], part), 71), part),
        "key_vecs": draw_key_vecs(jax.random.fold_in(jax.random.fold_in(keys[7], part), 71), part),
        "value_vecs": centred(part_keys[2], (2, SEQ_LEN, HE), 1.0, 6.0, ((0, 2), (1, 4))),
        "hidden_in": centred(part_keys[3], (2, SEQ_LEN, D), 0.5, 4.0, ((0, 2), (1, 4))),
        "out_proj": centred(keys[4], (2, HE, D), HE ** -0.5, 0.125, ((0, 2), (1, 4))),
        "couple_proj": centred(keys[5], (2, D, D), D ** -0.5, 0.125, ((0, 2), (1, 4))),
        "grad_mixed": centred(part_keys[6], (2, SEQ_LEN, D), 1.0, 6.0, ((0, 2), (1, 4))),
    }


def contract(left, right, left_dim, right_dim):
    return lax.dot_general(left, right, (((left_dim,), (right_dim,)), ((), ())), preferred_element_type=jnp.float32)

def softmax_weights(query_item, key_item, factor):
    scores = contract(query_item, key_item, 1, 1) * factor
    row_max = lax.optimization_barrier(jnp.max(scores, axis=-1, keepdims=True))
    raised = jnp.exp(scores - row_max)
    return raised / lax.optimization_barrier(jnp.sum(raised, axis=-1, keepdims=True))

def forward_item(bundle, factor):
    query_item, key_item, value_item = bundle
    weights = softmax_weights(query_item, key_item, factor)
    return contract(weights.astype(jnp.bfloat16), value_item, 1, 0).astype(jnp.bfloat16)

def backward_item(bundle, factor):
    query_item, key_item, value_item, grad_item = bundle
    weights = softmax_weights(query_item, key_item, factor)
    weights_low = weights.astype(jnp.bfloat16)
    grad_weights = contract(grad_item, value_item, 1, 1)
    row_dot = lax.optimization_barrier(jnp.sum(weights * grad_weights, axis=-1, keepdims=True))
    d_scores = (weights * (grad_weights - row_dot)).astype(jnp.bfloat16)
    grad_query = (contract(d_scores, key_item, 1, 0) * factor).astype(jnp.bfloat16)
    grad_key = (contract(d_scores, query_item, 0, 0) * factor).astype(jnp.bfloat16)
    grad_value = contract(weights_low, grad_item, 0, 0).astype(jnp.bfloat16)
    return (grad_query, grad_key, grad_value)

def to_items(whole):
    return whole.reshape(2, SEQ_LEN, NH, HEAD).transpose(0, 2, 1, 3).reshape(2 * NH, SEQ_LEN, HEAD)

def from_items(items):
    return items.reshape(2, NH, SEQ_LEN, HEAD).transpose(0, 2, 1, 3).reshape(2, SEQ_LEN, NH * HEAD)

def reference(queries, key_vecs, value_vecs, hidden_in, out_proj, couple_proj, grad_mixed):
    factor = 1.0 / math.sqrt(HEAD)
    query_items = to_items(queries)
    key_items = to_items(key_vecs)
    value_items = to_items(value_vecs)
    attended = from_items(lax.map(lambda bundle: forward_item(bundle, factor), (query_items, key_items, value_items)))
    group_width = HGROUP * HEAD
    hidden_list = []
    for branch_index in range(2):
        summed = hidden_in[branch_index].astype(jnp.float32)
        for group_index in range(NH // HGROUP):
            lower = group_index * group_width
            term = contract(attended[branch_index][:, lower:lower + group_width], out_proj[branch_index][lower:lower + group_width], 1, 0)
            summed = summed + lax.optimization_barrier(term.astype(jnp.bfloat16)).astype(jnp.float32)
        hidden_list.append(lax.optimization_barrier(summed.astype(jnp.bfloat16)))
    mixed_list = []
    back_list = []
    for branch_index in range(2):
        partner = hidden_list[1 - branch_index]
        coupled = hidden_list[branch_index].astype(jnp.float32) + contract(partner, couple_proj[branch_index], 1, 0)
        mixed_list.append(coupled.astype(jnp.bfloat16))
        back = contract(grad_mixed[branch_index], couple_proj[branch_index], 1, 1).astype(jnp.bfloat16)
        back_list.append(lax.optimization_barrier(back))
    grad_hidden_list = []
    grad_att_list = []
    couple_list = []
    for branch_index in range(2):
        grad_tok = grad_mixed[branch_index]
        grad_hid = (grad_tok.astype(jnp.float32) + back_list[1 - branch_index].astype(jnp.float32)).astype(jnp.bfloat16)
        grad_hidden_list.append(grad_hid)
        grad_att_list.append(contract(grad_hid, out_proj[branch_index], 1, 1).astype(jnp.bfloat16))
        partner_blocks = hidden_list[1 - branch_index].reshape(N_SEQ, S_DEV, D)
        grad_blocks = grad_tok.reshape(N_SEQ, S_DEV, D)

        def add_block(running, pair):
            term = contract(pair[0], pair[1], 0, 0).astype(jnp.bfloat16)
            return (running + lax.optimization_barrier(term).astype(jnp.float32), 0)
        summed, unused = lax.scan(add_block, jnp.zeros((D, D), jnp.float32), (partner_blocks, grad_blocks))
        couple_list.append(summed)
    grad_attended = jnp.stack(grad_att_list)
    grad_q, grad_k, grad_v = lax.map(lambda bundle: backward_item(bundle, factor), (query_items, key_items, value_items, to_items(grad_attended)))
    return (jnp.stack(mixed_list), jnp.stack(grad_hidden_list), from_items(grad_q), from_items(grad_k), from_items(grad_v), jnp.stack(couple_list))
```

```python
import math

import jax
import jax.numpy as jnp
from jax import lax
from jax.sharding import PartitionSpec as P

HEAD = 128


def swapped(value, axis):
    pairs = [(source, source ^ 1) for source in range(lax.axis_size(axis))]
    return lax.ppermute(value, axis, pairs)


def contract(left, right, left_dim, right_dim):
    return lax.dot_general(
        left, right, (((left_dim,), (right_dim,)), ((), ())), preferred_element_type=jnp.float32
    )


def batched(left, right, left_dim, right_dim):
    return lax.dot_general(
        left, right, (((left_dim,), (right_dim,)), ((0,), (0,))), preferred_element_type=jnp.float32
    )


def heads(rows):
    return rows.reshape(rows.shape[0], -1, HEAD).transpose(1, 0, 2)


def rows_of(items):
    return items.transpose(1, 0, 2).reshape(items.shape[1], -1)


def on_device(queries, key_vecs, value_vecs, hidden_in, out_proj, couple_proj, grad_mixed):
    factor = 1.0 / math.sqrt(HEAD)
    bf16 = jnp.bfloat16
    tok = queries.shape[1]
    me = lax.axis_index("seq")
    wide = couple_proj.shape[1]
    out_local, couple = out_proj[0], couple_proj[0]
    gm_all = lax.all_gather(grad_mixed[0], "seq", axis=0, tiled=True)
    stacked = jnp.concatenate([queries, key_vecs, value_vecs], axis=0)
    moved = lax.all_to_all(stacked, "seq", split_axis=2, concat_axis=1, tiled=True)
    q, k, v = heads(moved[0]), heads(moved[1]), heads(moved[2])
    back = contract(gm_all, couple, 1, 1).astype(bf16)
    back_all = lax.all_gather(swapped(back, "branch"), "seq", axis=1, tiled=True)
    scores = batched(q, k, 2, 2) * factor
    raised = jnp.exp(scores - jnp.max(scores, axis=-1, keepdims=True))
    weights = raised / jnp.sum(raised, axis=-1, keepdims=True)
    weights_low = weights.astype(bf16)
    attended = rows_of(batched(weights_low, v, 2, 1).astype(bf16))
    term = contract(attended, out_local, 1, 0)
    mine = lax.dynamic_slice_in_dim(term, me * tok, tok, 0) + hidden_in[0].astype(jnp.float32)
    term = lax.dynamic_update_slice_in_dim(term, mine, me * tok, 0).astype(bf16)
    hidden = lax.psum_scatter(term, "seq", scatter_dimension=1, tiled=True)
    partner = swapped(hidden, "branch")
    mixed = contract(partner, couple, 1, 0)
    own = lax.dynamic_slice_in_dim(mixed, me * wide, wide, 1) + hidden.astype(jnp.float32)
    mixed = lax.dynamic_update_slice_in_dim(mixed, own, me * wide, 1).astype(bf16)
    mixed_out = lax.psum_scatter(mixed, "seq", scatter_dimension=0, tiled=True)
    grad_cpl = contract(partner, gm_all, 0, 0)
    grad_hid = (gm_all.astype(jnp.float32) + back_all.astype(jnp.float32)).astype(bf16)
    grad_mine = lax.dynamic_slice_in_dim(grad_hid, me * tok, tok, 0)
    head_grad = heads(contract(grad_hid, out_local, 1, 1).astype(bf16))
    grad_w = batched(head_grad, v, 2, 2)
    row_dot = jnp.sum(weights * grad_w, axis=-1, keepdims=True)
    d_scores = (weights * (grad_w - row_dot)).astype(bf16)
    gq = rows_of((batched(d_scores, k, 2, 1) * factor).astype(bf16))
    gk = rows_of((batched(d_scores, q, 1, 1) * factor).astype(bf16))
    gv = rows_of(batched(weights_low, head_grad, 1, 1).astype(bf16))
    out = lax.all_to_all(jnp.stack([gq, gk, gv]), "seq", split_axis=1, concat_axis=2, tiled=True)
    return (mixed_out[None], grad_mine[None], out[0:1], out[1:2], out[2:3], grad_cpl[None])


def solution(mesh):
    token = P("branch", ("rep", "seq"), None)
    weight = P("branch", "seq", None)
    return jax.shard_map(
        on_device,
        mesh=mesh,
        in_specs=(token, token, token, token, weight, weight, token),
        out_specs=(token, token, token, token, token, P("branch", "seq", "rep")),
        check_vma=False,
    )
```

```python
import functools
import math

import jax
import jax.numpy as jnp
from jax import lax
from jax.experimental import pallas as pl
from jax.experimental.pallas import tpu as pltpu
from jax.sharding import PartitionSpec as P

HEAD = 128
ROWS = 256
BF16 = jnp.bfloat16
F32 = jnp.float32
MESH = pl.DeviceIdType.MESH
GM, Q, K, V, BACK, TERM, MIX, GQ, GK, GV, HID, KINDS = range(12)


def dot(left, right, left_dim, right_dim):
    return lax.dot_general(
        left, right, (((left_dim,), (right_dim,)), ((), ())), preferred_element_type=F32
    )


def kernel(
    n, q, k, v, hin, wo, wc, gm,
    mixed_o, gh_o, gq_o, gk_o, gv_o, gc_o,
    hq, hk, hv, gm_all, back, bc_all, att, wts, term, term_in, hid, hid_own,
    hg, gq, gk, gv, gk_acc, gv_acc, mix, mix_own, mix_in, send_sem, recv_sem,
):
    me = lax.axis_index("seq")
    mine = lax.axis_index("branch")
    other = 1 - mine
    tok, dim = gm.shape
    width = wc.shape[0]
    head_width = wo.shape[0]
    total = n * tok
    tile = min(ROWS, total)
    factor = 1.0 / math.sqrt(HEAD)

    def at(index, size):
        return pl.ds(pl.multiple_of(index * size, size), size)

    def to(step):
        return lax.rem(me + step, n)

    def source(step):
        return lax.rem(me - step + n, n)

    def copy(kind, step, src, dst, branch):
        return pltpu.make_async_remote_copy(
            src_ref=src,
            dst_ref=dst,
            send_sem=send_sem.at[kind, step],
            recv_sem=recv_sem.at[kind, step],
            device_id={"branch": branch, "seq": to(step)},
            device_id_type=MESH,
        )

    barrier = pltpu.get_barrier_semaphore()
    for step in range(n):
        pl.semaphore_signal(
            barrier, inc=1, device_id={"branch": other, "seq": to(step)}, device_id_type=MESH
        )
        if step:
            pl.semaphore_signal(
                barrier, inc=1, device_id={"branch": mine, "seq": to(step)}, device_id_type=MESH
            )
    pl.semaphore_wait(barrier, 2 * n - 1)

    gm_copies = [copy(GM, d, gm, gm_all.at[at(me, tok), :], mine) for d in range(1, n)]
    head_copies = [
        copy(kind, d, ref.at[:, at(to(d), head_width)], held.at[at(me, tok), :], mine)
        for kind, ref, held in ((Q, q, hq), (K, k, hk), (V, v, hv))
        for d in range(1, n)
    ]
    for c in gm_copies:
        c.start()
    for c in head_copies:
        c.start()
    gm_all[at(me, tok), :] = gm[...]
    for ref, held in ((q, hq), (k, hk), (v, hv)):
        held[at(me, tok), :] = ref[:, at(me, head_width)]

    for d in range(n):
        if d:
            gm_copies[d - 1].wait_recv()
        rows = at(source(d), tok)
        back[rows, :] = dot(gm_all[rows, :], wc[...], 1, 1).astype(BF16)
    back_copies = [
        copy(BACK, d, back, bc_all.at[:, at(me, width)], other) for d in range(n)
    ]
    for d in list(range(1, n)) + [0]:
        back_copies[d].start()

    for c in head_copies:
        c.wait_recv()

    def forward(index, carry):
        head = index // (total // tile)
        rows = at(index % (total // tile), tile)
        cols = at(head, HEAD)
        scores = dot(hq[rows, cols], hk[:, cols], 1, 1) * factor
        raised = jnp.exp(scores - jnp.max(scores, axis=-1, keepdims=True))
        weights = raised / jnp.sum(raised, axis=-1, keepdims=True)
        wts[head, rows, :] = weights
        att[rows, cols] = dot(weights.astype(BF16), hv[:, cols], 1, 0).astype(BF16)
        return carry

    heads = head_width // HEAD
    lax.fori_loop(0, heads * (total // tile), forward, 0)

    term_copies = [
        copy(TERM, d, term.at[:, at(to(d), width)], term_in.at[me], other) for d in range(n)
    ]
    own_rows = at(me, tok)
    for d in list(range(1, n)) + [0]:
        cols = at(to(d), width)

        def term_rows(index, carry, cols=cols):
            rows = at(index, tile)
            term[rows, cols] = dot(att[rows, :], wo[:, cols], 1, 0).astype(BF16)
            return carry

        lax.fori_loop(0, total // tile, term_rows, 0)
        term[own_rows, cols] = (
            dot(att[own_rows, :], wo[:, cols], 1, 0) + hin[:, cols].astype(F32)
        ).astype(BF16)
        term_copies[d].start()

    for c in back_copies:
        c.wait_recv()

    def head_grad(index, carry):
        rows = at(index, tok)
        grad = (gm_all[rows, :].astype(F32) + bc_all[rows, :].astype(F32)).astype(BF16)
        hg[rows, :] = dot(grad, wo[...], 1, 1).astype(BF16)
        return carry

    lax.fori_loop(0, n, head_grad, 0)
    gh_o[...] = (gm[...].astype(F32) + bc_all[own_rows, :].astype(F32)).astype(BF16)

    def backward(head, carry):
        cols = at(head, HEAD)
        for t in range(total // tile):
            rows = pl.ds(t * tile, tile)
            weights = wts[head, rows, :]
            grad = hg[rows, cols]
            grad_w = dot(grad, hv[:, cols], 1, 1)
            row_dot = jnp.sum(weights * grad_w, axis=-1, keepdims=True)
            d_scores = (weights * (grad_w - row_dot)).astype(BF16)
            gq[rows, cols] = (dot(d_scores, hk[:, cols], 1, 0) * factor).astype(BF16)
            part_k = dot(d_scores, hq[rows, cols], 0, 0)
            part_v = dot(weights.astype(BF16), grad, 0, 0)
            if t == 0:
                gk_acc[...] = part_k
                gv_acc[...] = part_v
            else:
                gk_acc[...] += part_k
                gv_acc[...] += part_v
        gk[:, cols] = (gk_acc[...] * factor).astype(BF16)
        gv[:, cols] = gv_acc[...].astype(BF16)
        return carry

    lax.fori_loop(0, heads, backward, 0)
    grads = ((GQ, gq, gq_o), (GK, gk, gk_o), (GV, gv, gv_o))
    grad_copies = [
        copy(kind, d, ref.at[at(to(d), tok), :], out.at[:, at(me, head_width)], mine)
        for kind, ref, out in grads
        for d in range(1, n)
    ]
    for c in grad_copies:
        c.start()
    for _, ref, out in grads:
        out[:, at(me, head_width)] = ref[own_rows, :]

    for c in term_copies:
        c.wait_recv()

    def add_terms(index, carry):
        rows = at(index, tok)
        summed = term_in[0, rows, :].astype(F32)
        for s in range(1, n):
            summed = summed + term_in[s, rows, :].astype(F32)
        hid[rows, :] = summed.astype(BF16)
        return carry

    lax.fori_loop(0, n, add_terms, 0)
    hid_copy = copy(HID, 0, hid, hid_own, other)
    hid_copy.start()
    mix_copies = [
        copy(MIX, d, mix.at[at(to(d), tok), :], mix_in.at[d - 1], mine) for d in range(1, n)
    ]
    own_cols = at(me, width)
    for d in list(range(1, n)) + [0]:
        rows = at(to(d), tok)
        mix_own[...] = dot(hid[rows, :], wc[...], 1, 0)
        if d == 1 or n == 1:
            hid_copy.wait_recv()
        mix_own[:, own_cols] += hid_own[rows, :].astype(F32)
        if d:
            mix[rows, :] = mix_own[...].astype(BF16)
            mix_copies[d - 1].start()

    def couple_grad(index, carry):
        cols = at(index, width)
        gc_o[:, cols] = dot(hid[...], gm_all[:, cols], 0, 0)
        return carry

    lax.fori_loop(0, dim // width, couple_grad, 0)
    for c in grad_copies:
        c.wait_recv()
    for c in mix_copies:
        c.wait_recv()
    summed = mix_own[...]
    for d in range(1, n):
        summed = summed + mix_in[d - 1].astype(F32)
    mixed_o[...] = summed.astype(BF16)
    for c in gm_copies + head_copies + back_copies + term_copies + grad_copies + mix_copies:
        c.wait_send()
    hid_copy.wait_send()


def on_device(queries, key_vecs, value_vecs, hidden_in, out_proj, couple_proj, grad_mixed):
    n = lax.axis_size("seq")
    tok, dim = grad_mixed.shape[1:]
    width = couple_proj.shape[1]
    head_width = out_proj.shape[1]
    wide = queries.shape[2]
    total = n * tok
    heads = head_width // HEAD
    item = pltpu.VMEM((total, head_width), BF16)
    whole = pltpu.VMEM((total, dim), BF16)
    slab = pltpu.VMEM((total, width), BF16)
    outs = pl.pallas_call(
        functools.partial(kernel, n),
        out_shape=[jax.ShapeDtypeStruct((tok, dim), BF16)] * 2
        + [jax.ShapeDtypeStruct((tok, wide), BF16)] * 3
        + [jax.ShapeDtypeStruct((width, dim), F32)],
        in_specs=[pl.BlockSpec(memory_space=pltpu.VMEM)] * 7,
        out_specs=[pl.BlockSpec(memory_space=pltpu.VMEM)] * 6,
        scratch_shapes=[
            item, item, item, whole, slab, whole, item,
            pltpu.VMEM((heads, total, total), F32),
            whole, pltpu.VMEM((n, total, width), BF16), slab, slab,
            item, item, item, item,
            pltpu.VMEM((total, HEAD), F32), pltpu.VMEM((total, HEAD), F32),
            whole, pltpu.VMEM((tok, dim), F32), pltpu.VMEM((max(n - 1, 1), tok, dim), BF16),
            pltpu.SemaphoreType.DMA((KINDS, n)), pltpu.SemaphoreType.DMA((KINDS, n)),
        ],
        compiler_params=pltpu.CompilerParams(
            collective_id=0, has_side_effects=True, vmem_limit_bytes=58 * 1024 * 1024
        ),
    )(
        queries[0], key_vecs[0], value_vecs[0], hidden_in[0], out_proj[0], couple_proj[0],
        grad_mixed[0],
    )
    return tuple(value[None] for value in outs)


def solution(mesh):
    token = P("branch", ("rep", "seq"), None)
    weight = P("branch", "seq", None)
    return jax.shard_map(
        on_device,
        mesh=mesh,
        in_specs=(token, token, token, token, weight, weight, token),
        out_specs=(token, token, token, token, token, P("branch", "seq", "rep")),
        check_vma=False,
    )
```

```python
import functools
import math

import jax
import jax.numpy as jnp
from jax import lax
from jax.experimental import pallas as pl
from jax.experimental.pallas import tpu as pltpu
from jax.sharding import PartitionSpec as P

HEAD = 128
ROWS = 256
PIECES = 4
BF16 = jnp.bfloat16
F32 = jnp.float32
MESH = pl.DeviceIdType.MESH
GM, Q, K, V, BACK, TERM, MIX, GQ, GK, GV, HID, KINDS = range(12)


def dot(left, right, left_dim, right_dim):
    return lax.dot_general(
        left, right, (((left_dim,), (right_dim,)), ((), ())), preferred_element_type=F32
    )


def kernel(
    n, q, k, v, hin, wo_hbm, wc_hbm, gm,
    mixed_o, gh_o, gq_o, gk_o, gv_o, gc_hbm,
    hq, hk, hv, gm_all, back, bc_all, att, wts, term, term_in, hid, hid_own,
    hg, gq, gk, gv, gk_acc, gv_acc, mix, mix_own, mix_in, wo, wc, gc_o,
    send_sem, recv_sem, load_sem,
):
    me = lax.axis_index("seq")
    mine = lax.axis_index("branch")
    other = 1 - mine
    tok, dim = gm.shape
    width = wc.shape[0]
    head_width = wo.shape[0]
    total = n * tok
    tile = min(ROWS, total)
    factor = 1.0 / math.sqrt(HEAD)

    def at(index, size):
        return pl.ds(pl.multiple_of(index * size, size), size)

    def to(step):
        return lax.rem(me + step, n)

    def source(step):
        return lax.rem(me - step + n, n)

    def copy(kind, step, src, dst, branch):
        return pltpu.make_async_remote_copy(
            src_ref=src,
            dst_ref=dst,
            send_sem=send_sem.at[kind, step],
            recv_sem=recv_sem.at[kind, step],
            device_id={"branch": branch, "seq": to(step)},
            device_id_type=MESH,
        )

    barrier = pltpu.get_barrier_semaphore()
    for step in range(n):
        pl.semaphore_signal(
            barrier, inc=1, device_id={"branch": other, "seq": to(step)}, device_id_type=MESH
        )
        if step:
            pl.semaphore_signal(
                barrier, inc=1, device_id={"branch": mine, "seq": to(step)}, device_id_type=MESH
            )
    pl.semaphore_wait(barrier, 2 * n - 1)

    gm_copies = [copy(GM, d, gm, gm_all.at[at(me, tok), :], mine) for d in range(1, n)]
    head_copies = [
        copy(kind, d, ref.at[:, at(to(d), head_width)], held.at[at(me, tok), :], mine)
        for kind, ref, held in ((Q, q, hq), (K, k, hk), (V, v, hv))
        for d in range(1, n)
    ]
    for c in head_copies:
        c.start()
    wo_load = pltpu.make_async_copy(wo_hbm, wo, load_sem.at[0])
    wc_load = pltpu.make_async_copy(wc_hbm, wc, load_sem.at[1])
    wo_load.start()
    wc_load.start()
    gm_all[at(me, tok), :] = gm[...]
    for ref, held in ((q, hq), (k, hk), (v, hv)):
        held[at(me, tok), :] = ref[:, at(me, head_width)]

    for c in head_copies[: 2 * (n - 1)]:
        c.wait_recv()
    for c in gm_copies:
        c.start()
    for c in head_copies[2 * (n - 1) :]:
        c.wait_recv()

    def forward(index, carry):
        head = index // (total // tile)
        rows = at(index % (total // tile), tile)
        cols = at(head, HEAD)
        scores = dot(hq[rows, cols], hk[:, cols], 1, 1) * factor
        raised = jnp.exp(scores - jnp.max(scores, axis=-1, keepdims=True))
        weights = raised / jnp.sum(raised, axis=-1, keepdims=True)
        wts[head, rows, :] = weights
        att[rows, cols] = dot(weights.astype(BF16), hv[:, cols], 1, 0).astype(BF16)
        return carry

    heads = head_width // HEAD
    lax.fori_loop(0, heads * (total // tile), forward, 0)

    wo_load.wait()
    term_copies = [
        copy(TERM, d, term.at[:, at(to(d), width)], term_in.at[me], other) for d in range(n)
    ]
    own_rows = at(me, tok)
    for d in list(range(1, n)) + [0]:
        cols = at(to(d), width)

        def term_rows(index, carry, cols=cols):
            rows = at(index, tile)
            term[rows, cols] = dot(att[rows, :], wo[:, cols], 1, 0).astype(BF16)
            return carry

        lax.fori_loop(0, total // tile, term_rows, 0)
        term[own_rows, cols] = (
            dot(att[own_rows, :], wo[:, cols], 1, 0) + hin[:, cols].astype(F32)
        ).astype(BF16)
        term_copies[d].start()

    wc_load.wait()
    for d in range(n):
        if d:
            gm_copies[d - 1].wait_recv()
        rows = at(source(d), tok)
        back[rows, :] = dot(gm_all[rows, :], wc[...], 1, 1).astype(BF16)
    back_copies = [
        copy(BACK, d, back, bc_all.at[:, at(me, width)], other) for d in range(n)
    ]
    for d in list(range(1, n)) + [0]:
        back_copies[d].start()

    for c in term_copies:
        c.wait_recv()

    def add_terms(index, carry):
        rows = at(index, tok)
        summed = term_in[0, rows, :].astype(F32)
        for s in range(1, n):
            summed = summed + term_in[s, rows, :].astype(F32)
        hid[rows, :] = summed.astype(BF16)
        return carry

    lax.fori_loop(0, n, add_terms, 0)
    hid_copy = copy(HID, 0, hid, hid_own, other)
    hid_copy.start()
    mix_copies = [
        copy(MIX, d, mix.at[at(to(d), tok), :], mix_in.at[d - 1], mine) for d in range(1, n)
    ]
    own_cols = at(me, width)
    for d in list(range(1, n)) + [0]:
        rows = at(to(d), tok)
        mix_own[...] = dot(hid[rows, :], wc[...], 1, 0)
        if d == 1 or n == 1:
            hid_copy.wait_recv()
        mix_own[:, own_cols] += hid_own[rows, :].astype(F32)
        if d:
            mix[rows, :] = mix_own[...].astype(BF16)

    for c in back_copies:
        c.wait_recv()
    for c in mix_copies:
        c.start()

    def head_grad(index, carry):
        rows = at(index, tok)
        grad = (gm_all[rows, :].astype(F32) + bc_all[rows, :].astype(F32)).astype(BF16)
        hg[rows, :] = dot(grad, wo[...], 1, 1).astype(BF16)
        return carry

    lax.fori_loop(0, n, head_grad, 0)
    gh_o[...] = (gm[...].astype(F32) + bc_all[own_rows, :].astype(F32)).astype(BF16)

    def backward(head, carry):
        cols = at(head, HEAD)
        for t in range(total // tile):
            rows = pl.ds(t * tile, tile)
            weights = wts[head, rows, :]
            grad = hg[rows, cols]
            grad_w = dot(grad, hv[:, cols], 1, 1)
            row_dot = jnp.sum(weights * grad_w, axis=-1, keepdims=True)
            d_scores = (weights * (grad_w - row_dot)).astype(BF16)
            gq[rows, cols] = (dot(d_scores, hk[:, cols], 1, 0) * factor).astype(BF16)
            part_k = dot(d_scores, hq[rows, cols], 0, 0)
            part_v = dot(weights.astype(BF16), grad, 0, 0)
            if t == 0:
                gk_acc[...] = part_k
                gv_acc[...] = part_v
            else:
                gk_acc[...] += part_k
                gv_acc[...] += part_v
        gk[:, cols] = (gk_acc[...] * factor).astype(BF16)
        gv[:, cols] = gv_acc[...].astype(BF16)
        return carry

    lax.fori_loop(0, heads, backward, 0)
    grads = ((GQ, gq, gq_o), (GK, gk, gk_o), (GV, gv, gv_o))
    grad_copies = [
        copy(kind, d, ref.at[at(to(d), tok), :], out.at[:, at(me, head_width)], mine)
        for kind, ref, out in grads
        for d in range(1, n)
    ]
    for c in grad_copies:
        c.start()
    for _, ref, out in grads:
        out[:, at(me, head_width)] = ref[own_rows, :]

    def couple_grad(index, carry):
        cols = at(index, width)
        gc_o[:, cols] = dot(hid[...], gm_all[:, cols], 0, 0)
        return carry

    lax.fori_loop(0, dim // width, couple_grad, 0)
    gc_store = pltpu.make_async_copy(gc_o, gc_hbm, load_sem.at[2])
    gc_store.start()
    for c in mix_copies:
        c.wait_recv()
    summed = mix_own[...]
    for d in range(1, n):
        summed = summed + mix_in[d - 1].astype(F32)
    mixed_o[...] = summed.astype(BF16)
    for c in grad_copies:
        c.wait_recv()
    for c in gm_copies + head_copies + back_copies + term_copies + grad_copies + mix_copies:
        c.wait_send()
    hid_copy.wait_send()
    gc_store.wait()


def store_kernel(*refs):
    sems = refs[-1]
    copies = []
    for index in range(5):
        copies.append((refs[index], refs[index + 6]))
    rows = refs[5].shape[0] // PIECES
    for piece in range(PIECES):
        part = pl.ds(piece * rows, rows)
        copies.append((refs[5].at[part, :], refs[11].at[part, :]))
    copies = [
        pltpu.make_async_copy(src, dst, sems.at[index])
        for index, (src, dst) in enumerate(copies)
    ]
    for c in copies:
        c.start()
    for c in copies:
        c.wait()


def on_device(queries, key_vecs, value_vecs, hidden_in, out_proj, couple_proj, grad_mixed):
    n = lax.axis_size("seq")
    tok, dim = grad_mixed.shape[1:]
    width = couple_proj.shape[1]
    head_width = out_proj.shape[1]
    wide = queries.shape[2]
    total = n * tok
    heads = head_width // HEAD
    item = pltpu.VMEM((total, head_width), BF16)
    whole = pltpu.VMEM((total, dim), BF16)
    slab = pltpu.VMEM((total, width), BF16)
    vmem = pl.BlockSpec(memory_space=pltpu.VMEM)
    hbm = pl.BlockSpec(memory_space=pl.ANY)
    outs = pl.pallas_call(
        functools.partial(kernel, n),
        out_shape=[jax.ShapeDtypeStruct((tok, dim), BF16)] * 2
        + [jax.ShapeDtypeStruct((tok, wide), BF16)] * 3
        + [jax.ShapeDtypeStruct((width, dim), F32)],
        in_specs=[vmem] * 4 + [hbm] * 2 + [vmem],
        out_specs=[vmem] * 5 + [hbm],
        scratch_shapes=[
            item, item, item, whole, slab, whole, item,
            pltpu.VMEM((heads, total, total), F32),
            whole, pltpu.VMEM((n, total, width), BF16), slab, slab,
            item, item, item, item,
            pltpu.VMEM((total, HEAD), F32), pltpu.VMEM((total, HEAD), F32),
            whole, pltpu.VMEM((tok, dim), F32), pltpu.VMEM((max(n - 1, 1), tok, dim), BF16),
            pltpu.VMEM((head_width, dim), BF16), pltpu.VMEM((width, dim), BF16),
            pltpu.VMEM((width, dim), F32),
            pltpu.SemaphoreType.DMA((KINDS, n)), pltpu.SemaphoreType.DMA((KINDS, n)),
            pltpu.SemaphoreType.DMA((3,)),
        ],
        compiler_params=pltpu.CompilerParams(
            collective_id=0, has_side_effects=True, vmem_limit_bytes=58 * 1024 * 1024
        ),
    )(
        queries[0], key_vecs[0], value_vecs[0], hidden_in[0], out_proj[0], couple_proj[0],
        grad_mixed[0],
    )
    outs = pl.pallas_call(
        store_kernel,
        out_shape=[jax.ShapeDtypeStruct(value.shape, value.dtype) for value in outs],
        in_specs=[hbm] * 6,
        out_specs=[hbm] * 6,
        scratch_shapes=[pltpu.SemaphoreType.DMA((5 + PIECES,))],
    )(*outs)
    return tuple(value[None] for value in outs)


def solution(mesh):
    token = P("branch", ("rep", "seq"), None)
    weight = P("branch", "seq", None)
    return jax.shard_map(
        on_device,
        mesh=mesh,
        in_specs=(token, token, token, token, weight, weight, token),
        out_specs=(token, token, token, token, token, P("branch", "seq", "rep")),
        check_vma=False,
    )
```

```python
import functools
import math

import jax
import jax.numpy as jnp
from jax import lax
from jax.experimental import pallas as pl
from jax.experimental.pallas import tpu as pltpu
from jax.sharding import PartitionSpec as P

HEAD = 128
ROWS = 256
PIECES = 4
BF16 = jnp.bfloat16
F32 = jnp.float32
MESH = pl.DeviceIdType.MESH
GM, Q, K, V, BACK, TERM, MIX, GQ, GK, GV, HID, KINDS = range(12)


def dot(left, right, left_dim, right_dim):
    return lax.dot_general(
        left, right, (((left_dim,), (right_dim,)), ((), ())), preferred_element_type=F32
    )


def kernel(
    n, q, k, v, hin, wo_hbm, wc_hbm, gm,
    mixed_o, gh_o, gq_o, gk_o, gv_o, gc_hbm,
    hq, hk, hv, gm_all, back, bc_all, att, wts, term, term_in, hid, hid_own,
    hg, gq, gk, gv, gk_acc, gv_acc, mix, mix_own, mix_in, wo, wc, gc_o,
    send_sem, recv_sem, load_sem,
):
    me = lax.axis_index("seq")
    mine = lax.axis_index("branch")
    other = 1 - mine
    tok, dim = gm.shape
    width = wc.shape[0]
    head_width = wo.shape[0]
    total = n * tok
    tile = min(ROWS, total)
    factor = 1.0 / math.sqrt(HEAD)

    def at(index, size):
        return pl.ds(pl.multiple_of(index * size, size), size)

    def to(step):
        return lax.rem(me + step, n)

    def source(step):
        return lax.rem(me - step + n, n)

    def copy(kind, step, src, dst, branch):
        return pltpu.make_async_remote_copy(
            src_ref=src,
            dst_ref=dst,
            send_sem=send_sem.at[kind, step],
            recv_sem=recv_sem.at[kind, step],
            device_id={"branch": branch, "seq": to(step)},
            device_id_type=MESH,
        )

    barrier = pltpu.get_barrier_semaphore()
    for step in range(n):
        pl.semaphore_signal(
            barrier, inc=1, device_id={"branch": other, "seq": to(step)}, device_id_type=MESH
        )
        if step:
            pl.semaphore_signal(
                barrier, inc=1, device_id={"branch": mine, "seq": to(step)}, device_id_type=MESH
            )
    pl.semaphore_wait(barrier, 2 * n - 1)

    gm_copies = [copy(GM, d, gm, gm_all.at[at(me, tok), :], mine) for d in range(1, n)]
    head_copies = [
        copy(kind, d, ref.at[:, at(to(d), head_width)], held.at[at(me, tok), :], mine)
        for kind, ref, held in ((Q, q, hq), (K, k, hk), (V, v, hv))
        for d in range(1, n)
    ]
    for c in head_copies:
        c.start()
    wo_load = pltpu.make_async_copy(wo_hbm, wo, load_sem.at[0])
    wc_load = pltpu.make_async_copy(wc_hbm, wc, load_sem.at[1])
    wo_load.start()
    wc_load.start()
    gm_all[at(me, tok), :] = gm[...]
    for ref, held in ((q, hq), (k, hk), (v, hv)):
        held[at(me, tok), :] = ref[:, at(me, head_width)]

    for c in head_copies[: 2 * (n - 1)]:
        c.wait_recv()
    for c in gm_copies:
        c.start()
    for c in head_copies[2 * (n - 1) :]:
        c.wait_recv()

    def forward(index, carry):
        head = index // (total // tile)
        rows = at(index % (total // tile), tile)
        cols = at(head, HEAD)
        scores = dot(hq[rows, cols], hk[:, cols], 1, 1) * factor
        raised = jnp.exp(scores - jnp.max(scores, axis=-1, keepdims=True))
        weights = raised / jnp.sum(raised, axis=-1, keepdims=True)
        wts[head, rows, :] = weights
        att[rows, cols] = dot(weights.astype(BF16), hv[:, cols], 1, 0).astype(BF16)
        return carry

    heads = head_width // HEAD
    lax.fori_loop(0, heads * (total // tile), forward, 0)

    wo_load.wait()
    term_copies = [
        copy(TERM, d, term.at[:, at(to(d), width)], term_in.at[me], other) for d in range(n)
    ]
    own_rows = at(me, tok)
    for d in list(range(1, n)) + [0]:
        cols = at(to(d), width)

        def term_rows(index, carry, cols=cols):
            rows = at(index, tile)
            term[rows, cols] = dot(att[rows, :], wo[:, cols], 1, 0).astype(BF16)
            return carry

        lax.fori_loop(0, total // tile, term_rows, 0)
        term[own_rows, cols] = (
            dot(att[own_rows, :], wo[:, cols], 1, 0) + hin[:, cols].astype(F32)
        ).astype(BF16)
        term_copies[d].start()

    wc_load.wait()
    for d in range(n):
        if d:
            gm_copies[d - 1].wait_recv()
        rows = at(source(d), tok)
        back[rows, :] = dot(gm_all[rows, :], wc[...], 1, 1).astype(BF16)
    back_copies = [
        copy(BACK, d, back, bc_all.at[:, at(me, width)], other) for d in range(n)
    ]
    for d in list(range(1, n)) + [0]:
        back_copies[d].start()

    for c in term_copies:
        c.wait_recv()

    def add_terms(index, carry):
        rows = at(index, tok)
        summed = term_in[0, rows, :].astype(F32)
        for s in range(1, n):
            summed = summed + term_in[s, rows, :].astype(F32)
        hid[rows, :] = summed.astype(BF16)
        return carry

    lax.fori_loop(0, n, add_terms, 0)
    hid_copy = copy(HID, 0, hid, hid_own, other)
    hid_copy.start()
    mix_copies = [
        copy(MIX, d, mix.at[at(to(d), tok), :], mix_in.at[d - 1], mine) for d in range(1, n)
    ]
    own_cols = at(me, width)
    for d in list(range(1, n)) + [0]:
        rows = at(to(d), tok)
        mix_own[...] = dot(hid[rows, :], wc[...], 1, 0)
        if d == 1 or n == 1:
            hid_copy.wait_recv()
        mix_own[:, own_cols] += hid_own[rows, :].astype(F32)
        if d:
            mix[rows, :] = mix_own[...].astype(BF16)

    for c in back_copies:
        c.wait_recv()
    for c in mix_copies:
        c.start()

    def head_grad(index, carry):
        rows = at(index, tok)
        grad = (gm_all[rows, :].astype(F32) + bc_all[rows, :].astype(F32)).astype(BF16)
        hg[rows, :] = dot(grad, wo[...], 1, 1).astype(BF16)
        return carry

    lax.fori_loop(0, n, head_grad, 0)
    gh_o[...] = (gm[...].astype(F32) + bc_all[own_rows, :].astype(F32)).astype(BF16)

    def backward(head, carry):
        cols = at(head, HEAD)
        for t in range(total // tile):
            rows = pl.ds(t * tile, tile)
            weights = wts[head, rows, :]
            grad = hg[rows, cols]
            grad_w = dot(grad, hv[:, cols], 1, 1)
            row_dot = jnp.sum(weights * grad_w, axis=-1, keepdims=True)
            d_scores = (weights * (grad_w - row_dot)).astype(BF16)
            gq[rows, cols] = (dot(d_scores, hk[:, cols], 1, 0) * factor).astype(BF16)
            part_k = dot(d_scores, hq[rows, cols], 0, 0)
            part_v = dot(weights.astype(BF16), grad, 0, 0)
            if t == 0:
                gk_acc[...] = part_k
                gv_acc[...] = part_v
            else:
                gk_acc[...] += part_k
                gv_acc[...] += part_v
        gk[:, cols] = (gk_acc[...] * factor).astype(BF16)
        gv[:, cols] = gv_acc[...].astype(BF16)
        return carry

    lax.fori_loop(0, heads, backward, 0)
    grads = ((GQ, gq, gq_o), (GK, gk, gk_o), (GV, gv, gv_o))
    grad_copies = [
        copy(kind, d, ref.at[at(to(d), tok), :], out.at[:, at(me, head_width)], mine)
        for kind, ref, out in grads
        for d in range(1, n)
    ]
    for c in grad_copies:
        c.start()
    for _, ref, out in grads:
        out[:, at(me, head_width)] = ref[own_rows, :]

    def couple_grad(index, carry):
        cols = at(index, width)
        gc_o[:, cols] = dot(hid[...], gm_all[:, cols], 0, 0)
        return carry

    lax.fori_loop(0, dim // width, couple_grad, 0)
    gc_store = pltpu.make_async_copy(gc_o, gc_hbm, load_sem.at[2])
    gc_store.start()
    for c in mix_copies:
        c.wait_recv()
    summed = mix_own[...]
    for d in range(1, n):
        summed = summed + mix_in[d - 1].astype(F32)
    mixed_o[...] = summed.astype(BF16)
    for c in grad_copies:
        c.wait_recv()
    for c in gm_copies + head_copies + back_copies + term_copies + grad_copies + mix_copies:
        c.wait_send()
    hid_copy.wait_send()
    gc_store.wait()


def store_kernel(*refs):
    values, outs, held = refs[:6], refs[6:12], refs[12:18]
    load_sem, store_sem = refs[18:]
    blocks = [(index, pl.ds(0, refs[index].shape[0])) for index in range(5)]
    rows = refs[5].shape[0] // PIECES
    blocks += [(5, pl.ds(piece * rows, rows)) for piece in range(PIECES)]
    loads, stores = [], []
    for place, (index, part) in enumerate(blocks):
        loads.append(
            pltpu.make_async_copy(
                values[index].at[part, :], held[index].at[part, :], load_sem.at[place]
            )
        )
        stores.append(
            pltpu.make_async_copy(
                held[index].at[part, :], outs[index].at[part, :], store_sem.at[place]
            )
        )
    for c in loads:
        c.start()
    for load, store in zip(loads, stores):
        load.wait()
        store.start()
    for c in stores:
        c.wait()


def on_device(queries, key_vecs, value_vecs, hidden_in, out_proj, couple_proj, grad_mixed):
    n = lax.axis_size("seq")
    tok, dim = grad_mixed.shape[1:]
    width = couple_proj.shape[1]
    head_width = out_proj.shape[1]
    wide = queries.shape[2]
    total = n * tok
    heads = head_width // HEAD
    item = pltpu.VMEM((total, head_width), BF16)
    whole = pltpu.VMEM((total, dim), BF16)
    slab = pltpu.VMEM((total, width), BF16)
    vmem = pl.BlockSpec(memory_space=pltpu.VMEM)
    hbm = pl.BlockSpec(memory_space=pl.ANY)
    outs = pl.pallas_call(
        functools.partial(kernel, n),
        out_shape=[jax.ShapeDtypeStruct((tok, dim), BF16)] * 2
        + [jax.ShapeDtypeStruct((tok, wide), BF16)] * 3
        + [jax.ShapeDtypeStruct((width, dim), F32)],
        in_specs=[vmem] * 4 + [hbm] * 2 + [vmem],
        out_specs=[vmem] * 5 + [hbm],
        scratch_shapes=[
            item, item, item, whole, slab, whole, item,
            pltpu.VMEM((heads, total, total), F32),
            whole, pltpu.VMEM((n, total, width), BF16), slab, slab,
            item, item, item, item,
            pltpu.VMEM((total, HEAD), F32), pltpu.VMEM((total, HEAD), F32),
            whole, pltpu.VMEM((tok, dim), F32), pltpu.VMEM((max(n - 1, 1), tok, dim), BF16),
            pltpu.VMEM((head_width, dim), BF16), pltpu.VMEM((width, dim), BF16),
            pltpu.VMEM((width, dim), F32),
            pltpu.SemaphoreType.DMA((KINDS, n)), pltpu.SemaphoreType.DMA((KINDS, n)),
            pltpu.SemaphoreType.DMA((3,)),
        ],
        compiler_params=pltpu.CompilerParams(
            collective_id=0, has_side_effects=True, vmem_limit_bytes=58 * 1024 * 1024
        ),
    )(
        queries[0], key_vecs[0], value_vecs[0], hidden_in[0], out_proj[0], couple_proj[0],
        grad_mixed[0],
    )
    outs = pl.pallas_call(
        store_kernel,
        out_shape=[jax.ShapeDtypeStruct(value.shape, value.dtype) for value in outs],
        in_specs=[hbm] * 6,
        out_specs=[hbm] * 6,
        scratch_shapes=[pltpu.VMEM(value.shape, value.dtype) for value in outs]
        + [pltpu.SemaphoreType.DMA((5 + PIECES,))] * 2,
        compiler_params=pltpu.CompilerParams(vmem_limit_bytes=24 * 1024 * 1024),
    )(*outs)
    return tuple(value[None] for value in outs)


def solution(mesh):
    token = P("branch", ("rep", "seq"), None)
    weight = P("branch", "seq", None)
    return jax.shard_map(
        on_device,
        mesh=mesh,
        in_specs=(token, token, token, token, weight, weight, token),
        out_specs=(token, token, token, token, token, P("branch", "seq", "rep")),
        check_vma=False,
    )
```
